256 devices in a mesh: dp: 32 (over x, y, core), tensor: 8 (over z).
Axes of the slice: x: 4, y: 4, z: 8, core: 2. Of those that a mesh axis runs over, the one named last changes fastest.
Arguments:
- activations: bfloat16 [16384, 18432], P('dp', 'tensor'), may hold values from -36 to 36
- out_grad: bfloat16 [16384, 2304], P(('dp', 'tensor')), may hold values from -1.08 to 1.08
- accum: float32 [18432, 2304], P(('tensor', 'dp')), may hold values from -6 to 6
- noise: float32 [18432, 2304], P(('tensor', 'dp')), may hold values from -6 to 6
Outputs:
- noisy_sum: float32 [18432, 2304], P(('tensor', 'dp'))
- clip_factors: float32 [32], P('dp')
The draws below stay inside these ranges and needn't reach their ends.
All inputs are finite; a program needn't handle non-finite values.
Results may differ from the reference program's by a relative error of at most 0.0003.
Values may be sent and summed in bfloat16 or wider, within the bound.
A program may use at most 128 MiB of HBM per device.

```python
import math
import jax
import jax.numpy as jnp
from jax import lax

D = 2304
FF = 18432
LEN = 512
EXAMPLES = 32
TOKENS = 16384


def draw_activations(key, part):
    key = jax.random.fold_in(key, 11)
    key_val, key_col = jax.random.split(key)
    place = jnp.arange(FF, dtype=jnp.float32) / FF
    rough = jnp.exp(jax.random.uniform(key_col, (FF,), jnp.float32, math.log(0.3), math.log(3.0)))
    values = jax.random.truncated_normal(key_val, -6.0, 6.0, (TOKENS, FF), jnp.float32)
    trend = 2.0 ** place
    return (values * (trend * rough)[None, :]).astype(jnp.bfloat16)


def draw_out_grad(key, part):
    key = jax.random.fold_in(key, 12)
    key_val, key_ex, key_tok, key_col = jax.random.split(key, 4)
    example = jnp.exp(jax.random.uniform(key_ex, (EXAMPLES,), jnp.float32, math.log(0.002), math.log(0.02)))
    example_rows = jnp.repeat(example, LEN)
    token = jnp.exp(jax.random.uniform(key_tok, (TOKENS,), jnp.float32, math.log(0.3), math.log(3.0)))
    column = jnp.exp(jax.random.uniform(key_col, (D,), jnp.float32, math.log(0.3), math.log(3.0)))
    values = jax.random.truncated_normal(key_val, -6.0, 6.0, (TOKENS, D), jnp.float32)
    return (values * (example_rows * token)[:, None] * column[None, :]).astype(jnp.bfloat16)


def levels(key, extent, cuts, smallest, largest):
    gain = 1.0
    for dim, parts in cuts:
        heights = jax.random.uniform(jax.random.fold_in(jax.random.fold_in(key, 6), dim), (parts,), jnp.float32, smallest / len(cuts), largest / len(cuts))
        gain = gain * jnp.repeat(jnp.exp(heights), extent[dim] // parts).reshape((-1,) + (1,) * (len(extent) - 1 - dim))
    return gain


def scatter_about(rng, dims, scale, reach, shards=(), kind=jnp.bfloat16):
    entries = jax.random.normal(rng, dims, jnp.float32) * scale
    if len(shards) > 0:
        entries = levels(rng, dims, shards, -0.22, 0.18) * entries
    return jnp.clip(entries, min=-reach, max=reach).astype(kind)


def setup_inputs(seed: int = 0) -> dict:
    key_of = jax.random.split(jax.random.key(seed), 5)
    activations = draw_activations(jax.random.fold_in(key_of[4], 71), 0)
    out_grad = draw_out_grad(jax.random.fold_in(key_of[4], 71), 0)
    accum = scatter_about(key_of[2], (FF, D), 1.0, 6.0, ((0, 256),), jnp.float32)
    noise = scatter_about(key_of[3], (FF, D), 1.0, 6.0, ((0, 256),), jnp.float32)
    return {"activations": activations, "out_grad": out_grad, "accum": accum, "noise": noise}


def reference(activations, out_grad, accum, noise):
    bound = 0.02 * math.sqrt(LEN * FF * D)
    acts = activations.reshape(EXAMPLES, LEN, FF)
    grads = out_grad.reshape(EXAMPLES, LEN, D)

    def one_example(total, pair):
        hidden, upstream = pair
        act_gram = jnp.dot(hidden, hidden.T, preferred_element_type=jnp.float32)
        out_gram = jnp.dot(upstream, upstream.T, preferred_element_type=jnp.float32)
        sq_norm = jnp.sum(act_gram * out_gram)
        factor = jnp.minimum(1.0, bound / jnp.sqrt(sq_norm))
        product = jnp.dot(hidden.T, upstream, preferred_element_type=jnp.float32)
        return (total + factor * product, factor)
    start = jnp.zeros((FF, D), jnp.float32)
    total, factors = lax.scan(one_example, start, (acts, grads))
    return (accum + total + noise, factors)
```

```python
import functools
import math

import jax
import jax.numpy as jnp
from jax import lax
from jax.experimental import pallas as pl
from jax.experimental.pallas import tpu as pltpu
from jax.sharding import PartitionSpec as P

MESH = pl.DeviceIdType.MESH
LEN = 512
FF = 2304
D = 2304
HALF = D // 2
ROWS = 64
SUB = 16
NSUB = ROWS // SUB
CHUNK = 144
WIDTH = (640, 512)
START = (0, 640)
STEP = 48
TOP = 80

SLOT = ((0, 1, 3, 5, 7), (0, 2, 4, 6, 7))
SUBS = ((0, 1, 2, 3), (2, 3, 0, 1))
BLOCK = (0, -1, 1, -2, 2, -3, 3, 4)
GATHER = 3 * NSUB + NSUB // 2

ORDER = ((2, 3, 1, 0, 2, 3), (1, 0, 2, 3, 1, 0))

POWER = 9
REACH = 2.0**14


def encode(x, scale):
    y = x * scale
    y2 = y * y
    y4 = y2 * y2
    return (y4 * y4 * y).astype(jnp.bfloat16)


def decode(sent, unscale):
    z = sent.astype(jnp.float32)
    r = jnp.exp(jnp.log(jnp.abs(z)) * (1.0 / POWER)) * unscale
    return jnp.where(z < 0, -r, r)


def fold(prod):
    total = None
    for i in range(0, prod.shape[0], 8):
        for j in range(0, prod.shape[1], 128):
            piece = prod[i : i + 8, j : j + 128]
            total = piece if total is None else total + piece
    return total


def kernel(
    bound, h_hbm, g_hbm, acc_hbm, noise_hbm, out_ref, clip_ref,
    hs, hp, ht, gs, gp, t, gram, norm, norms, send0, send1, recv0, recv1, sum0, sum1, fin, swap, acc, noise,
    load_sem, gs_send, gs_recv, hp_send, hp_recv, gp_send, gp_recv, n_send, n_recv, rs_send, rs_recv, swap_sem,
):
    dp, z = lax.axis_index("dp"), lax.axis_index("tensor")
    x, y, c = dp // 8, (dp // 2) % 4, dp % 2
    o = 1 - c
    partner = (dp - c + o, z)
    along_z = ((dp, (z + 1) % 8), (dp, (z + 7) % 8))
    sends, recvs, sums = (send0, send1), (recv0, recv1), (sum0, sum1)

    ia = (x * o + y * c, y * o + x * c)
    ib = (ia[1], ia[0])
    step_a = (4 * o + c, o + 4 * c)
    step_b = (step_a[1], step_a[0])

    def chunk_of(part, a, b):
        return ((ia[part] + a + 4) % 4) * step_a[part] + ((ib[part] + b + 4) % 4) * step_b[part]

    def device_of(part, a, b):
        return (chunk_of(part, a, b) * 2 + c, z)

    loads = []
    for s in range(8):
        row = pl.multiple_of(((z + BLOCK[s] + 8) % 8) * ROWS, ROWS)
        loads.append(pltpu.make_async_copy(h_hbm.at[pl.ds(row, ROWS)], hs.at[pl.ds(s * ROWS, ROWS)], load_sem.at[s]))
    g_load = pltpu.make_async_copy(g_hbm, gs.at[pl.ds(0, ROWS)], load_sem.at[8])
    acc_load = pltpu.make_async_copy(acc_hbm, acc, load_sem.at[9])
    noise_load = pltpu.make_async_copy(noise_hbm, noise, load_sem.at[10])
    g_load.start()
    for copy in loads:
        copy.start()
    acc_load.start()
    noise_load.start()

    others = [(dp, (z + k) % 8) for k in range(1, 8)]
    others += [(partner[0], (z + k) % 8) for k in range(8)]
    others += [device_of(0, 1, 0), device_of(0, -1, 0), device_of(0, 0, 1), device_of(0, 0, -1)]
    barrier = pltpu.get_barrier_semaphore()
    for device in others:
        pl.semaphore_signal(barrier, inc=1, device_id=device, device_id_type=MESH)
    pl.semaphore_wait(barrier, len(others))

    def gather(way, n):
        sub = SUBS[way][n % NSUB]
        src = gs.at[pl.ds(SLOT[way][n // NSUB] * ROWS + sub * SUB, SUB)]
        dst = gs.at[pl.ds(SLOT[way][n // NSUB + 1] * ROWS + sub * SUB, SUB)]
        return pltpu.make_async_remote_copy(
            src_ref=src, dst_ref=dst, send_sem=gs_send.at[way, n], recv_sem=gs_recv.at[way, n],
            device_id=along_z[way], device_id_type=MESH,
        )

    def give_h(s):
        return pltpu.make_async_remote_copy(
            src_ref=hs.at[pl.ds(s * ROWS, ROWS)], dst_ref=hp.at[pl.ds(s * ROWS, ROWS)],
            send_sem=hp_send.at[s], recv_sem=hp_recv.at[s], device_id=partner, device_id_type=MESH,
        )

    mine = pl.ds(pl.multiple_of(c * HALF, 128), HALF)
    theirs = pl.ds(pl.multiple_of(o * HALF, 128), HALF)

    def give_g(s):
        return pltpu.make_async_remote_copy(
            src_ref=gs.at[pl.ds(s * ROWS, ROWS), theirs], dst_ref=gp.at[pl.ds(s * ROWS, ROWS)],
            send_sem=gp_send.at[s], recv_sem=gp_recv.at[s], device_id=partner, device_id_type=MESH,
        )

    g_load.wait()
    for n in range(NSUB):
        for way in range(2):
            gather(way, n).start()
    give_g(0).start()
    for s in range(8):
        loads[s].wait()
        give_h(s).start()

    def act_gram(i, _):
        r = pl.ds(pl.multiple_of(i * 128, 128), 128)
        gram[r, :] = lax.dot_general(
            hs[r, :], hs[...], (((1,), (1,)), ((), ())), preferred_element_type=jnp.float32
        )
        return 0

    def transpose(src, e):
        def body(i, _):
            r = pl.ds(pl.multiple_of(i * 128, 128), 128)
            ht[e, r, :] = src[:, r].T
            return 0

        lax.fori_loop(0, FF // 128, body, 0)

    def out_gram(lo, hi):
        prod = gram[lo:hi, 0:hi] * lax.dot_general(
            gs[lo:hi, :], gs[0:hi, :], (((1,), (1,)), ((), ())), preferred_element_type=jnp.float32
        )
        total = fold(prod[:, lo:hi])
        return total if lo == 0 else total + 2.0 * fold(prod[:, 0:lo])

    def terms(e, lo, first):
        def body(i, _):
            r = pl.ds(pl.multiple_of(i * 256, 256), 256)
            rhs = gs[lo : lo + 256, mine] if e == 0 else gp[lo : lo + 256, :]
            value = jnp.dot(ht[e, r, lo : lo + 256], rhs, preferred_element_type=jnp.float32)
            if first:
                t[e, r, :] = value
            else:
                t[e, r, :] += value
            return 0

        lax.fori_loop(0, FF // 256, body, 0)

    for n in range(GATHER):
        for way in range(2):
            gather(way, n).wait_recv()
            if n + NSUB < GATHER:
                gather(way, n + NSUB).start()
        if n % NSUB == NSUB - 1:
            for way in range(2):
                give_g(SLOT[way][n // NSUB + 1]).start()
        if n == 0:
            lax.fori_loop(0, 4, act_gram, 0)
        elif n == 1:
            transpose(hs, 0)
        elif n == 3:
            for s in range(8):
                give_h(s).wait_recv()
            transpose(hp, 1)
        elif n == 8:
            norm[...] = out_gram(0, 256)
            terms(0, 0, True)
        elif n == 9:
            for s in range(4):
                give_g(s).wait_recv()
            terms(1, 0, True)
        elif n == 11:
            norm[...] += out_gram(256, 384)
    give_g(7).start()

    norm[...] += out_gram(384, 512)

    def give_norm(e, k):
        device = (dp if e == 0 else partner[0], (z + k) % 8)
        return pltpu.make_async_remote_copy(
            src_ref=norm, dst_ref=norms.at[e, k], send_sem=n_send.at[e, k], recv_sem=n_recv.at[e, k],
            device_id=device, device_id_type=MESH,
        )

    pairs = [(e, k) for k in (4, 3, 5, 2, 6, 1, 7, 0) for e in range(2) if (e, k) != (0, 0)]
    for e, k in pairs:
        give_norm(e, k).start()
    terms(0, 256, False)
    for s in range(4, 8):
        give_g(s).wait_recv()
    terms(1, 256, False)
    for e, k in pairs:
        give_norm(e, k).wait_recv()

    def factor(e):
        total = norm[...] if e == 0 else norms[1, 0]
        for k in range(1, 8):
            total = total + norms[e, k]
        sq_norm = jnp.broadcast_to(jnp.sum(total), (8, 128))
        return jnp.max(jnp.minimum(1.0, bound / jnp.sqrt(sq_norm)))

    f0, f1 = factor(0), factor(1)
    clip_ref[0] = f0

    limit = 2.0 * bound
    scale = [REACH / (limit * chips) for chips in (1, 1, 2, 2, 2, 2, 4, 8)]

    def own(part, chunk, r):
        rows = pl.ds(pl.multiple_of(chunk * CHUNK + r, 16), STEP)
        cols = slice(START[part], START[part] + WIDTH[part])
        return f0 * t[0, rows, cols] + f1 * t[1, rows, cols]

    def over_rows(body):
        def step(i, _):
            r = pl.multiple_of(i * STEP, 16)
            body(r, pl.ds(r, STEP))
            return 0

        lax.fori_loop(0, CHUNK // STEP, step, 0)

    def message(part, way, slot):
        sign = 1 - 2 * way
        rows = pl.ds(0, CHUNK)
        if slot == 6:
            rows = pl.ds(0, TOP) if way == 0 else pl.ds(TOP, CHUNK - TOP)
        device = device_of(part, sign, 0) if slot < 6 else device_of(part, 0, sign)
        return pltpu.make_async_remote_copy(
            src_ref=sends[part].at[way, slot, rows], dst_ref=recvs[part].at[way, slot, rows],
            send_sem=rs_send.at[part, way, slot], recv_sem=rs_recv.at[part, way, slot],
            device_id=device, device_id_type=MESH,
        )

    def first_phase(part, way, slot):
        sign = 1 - 2 * way
        chunk = chunk_of(part, 2 if slot < 2 else sign, ORDER[way][slot])
        if slot >= 4:
            message(part, way, slot - 4).wait_recv()

        def body(r, rows):
            value = own(part, chunk, r)
            if slot >= 4:
                value += decode(recvs[part][way, slot - 4, rows, :], 1.0 / scale[slot - 4])
            sends[part][way, slot, rows, :] = encode(value, scale[slot])

        over_rows(body)
        message(part, way, slot).start()

    def take(part, way, slot):
        b = ORDER[way][slot]
        message(part, way, slot).wait_recv()

        def body(r, rows):
            sums[part][b, rows, :] += decode(recvs[part][way, slot, rows, :], 1.0 / scale[slot])

        over_rows(body)

    for slot in range(4):
        for way in range(2):
            for part in range(2):
                first_phase(part, way, slot)
    for part in range(2):
        for b in range(4):
            chunk = chunk_of(part, 0, b)

            def body(r, rows):
                sums[part][b, rows, :] = own(part, chunk, r)

            over_rows(body)
    for slot in (4, 5):
        for way in range(2):
            for part in range(2):
                first_phase(part, way, slot)
    for slot in (2, 3, 4):
        for way in range(2):
            for part in range(2):
                take(part, way, slot)

    for part in range(2):

        def body(r, rows):
            value = encode(sums[part][2, rows, :], scale[6])
            for way in range(2):
                sends[part][way, 6, rows, :] = value

        over_rows(body)
        for way in range(2):
            message(part, way, 6).start()

    def pass_on(part, way):
        b = 1 if way == 0 else 3
        rows = slice(0, TOP) if way == 0 else slice(TOP, CHUNK)
        message(part, way, 6).wait_recv()
        sums[part][b, rows, :] += decode(recvs[part][way, 6, rows, :], 1.0 / scale[6])

        def body(r, rows):
            sends[part][way, 7, rows, :] = encode(sums[part][b, rows, :], scale[7])

        over_rows(body)
        message(part, way, 7).start()

    for part in range(2):
        pass_on(part, 0)
    for way in range(2):
        for part in range(2):
            take(part, way, 5)
    for part in range(2):
        pass_on(part, 1)
    for part in range(2):
        for way in range(2):
            message(part, way, 7).wait_recv()
        cols = slice(START[part], START[part] + WIDTH[part])

        def body(r, rows):
            fin[rows, cols] = (
                sums[part][0, rows, :]
                + decode(recvs[part][0, 7, rows, :], 1.0 / scale[7])
                + decode(recvs[part][1, 7, rows, :], 1.0 / scale[7])
            )

        over_rows(body)

    my_rows = pl.ds(pl.multiple_of(c * (CHUNK // 2), 8), CHUNK // 2)
    their_rows = pl.ds(pl.multiple_of(o * (CHUNK // 2), 8), CHUNK // 2)
    exchange = pltpu.make_async_remote_copy(
        src_ref=fin.at[their_rows], dst_ref=swap, send_sem=swap_sem.at[0], recv_sem=swap_sem.at[1],
        device_id=partner, device_id_type=MESH,
    )
    exchange.start()
    acc_load.wait()
    noise_load.wait()
    out_ref[:, mine] = acc[:, mine] + fin[my_rows, :] + noise[:, mine]
    exchange.wait_recv()
    out_ref[:, theirs] = acc[:, theirs] + swap[...] + noise[:, theirs]

    exchange.wait_send()
    for way in range(2):
        for n in range(GATHER):
            gather(way, n).wait_send()
    for s in range(8):
        give_h(s).wait_send()
        give_g(s).wait_send()
    for e, k in pairs:
        give_norm(e, k).wait_send()
    for part in range(2):
        for way in range(2):
            for slot in range(8):
                message(part, way, slot).wait_send()


def local(activations, out_grad, accum, noise):
    hidden_all = activations.shape[1] * lax.axis_size("tensor")
    bound = 0.02 * math.sqrt(activations.shape[0] * hidden_all * out_grad.shape[1])
    f32, bf16, dma = jnp.float32, jnp.bfloat16, pltpu.SemaphoreType.DMA
    hbm = pl.BlockSpec(memory_space=pl.ANY)
    return pl.pallas_call(
        functools.partial(kernel, bound),
        out_shape=(jax.ShapeDtypeStruct(accum.shape, f32), jax.ShapeDtypeStruct((1,), f32)),
        in_specs=[hbm] * 4,
        out_specs=(pl.BlockSpec(memory_space=pltpu.VMEM), pl.BlockSpec(memory_space=pltpu.SMEM)),
        scratch_shapes=[
            pltpu.VMEM((LEN, FF), bf16),
            pltpu.VMEM((LEN, FF), bf16),
            pltpu.VMEM((2, FF, LEN), bf16),
            pltpu.VMEM((LEN, D), bf16),
            pltpu.VMEM((LEN, HALF), bf16),
            pltpu.VMEM((2, FF, HALF), f32),
            pltpu.VMEM((LEN, LEN), f32),
            pltpu.VMEM((8, 128), f32),
            pltpu.VMEM((2, 8, 8, 128), f32),
            pltpu.VMEM((2, 8, CHUNK, WIDTH[0]), bf16),
            pltpu.VMEM((2, 8, CHUNK, WIDTH[1]), bf16),
            pltpu.VMEM((2, 8, CHUNK, WIDTH[0]), bf16),
            pltpu.VMEM((2, 8, CHUNK, WIDTH[1]), bf16),
            pltpu.VMEM((4, CHUNK, WIDTH[0]), f32),
            pltpu.VMEM((4, CHUNK, WIDTH[1]), f32),
            pltpu.VMEM((CHUNK, HALF), f32),
            pltpu.VMEM((CHUNK // 2, HALF), f32),
            pltpu.VMEM(accum.shape, f32),
            pltpu.VMEM(accum.shape, f32),
            dma((11,)),
            dma((2, GATHER)),
            dma((2, GATHER)),
            dma((8,)),
            dma((8,)),
            dma((8,)),
            dma((8,)),
            dma((2, 8)),
            dma((2, 8)),
            dma((2, 2, 8)),
            dma((2, 2, 8)),
            dma((2,)),
        ],
        compiler_params=pltpu.CompilerParams(
            collective_id=0, has_side_effects=True, vmem_limit_bytes=62 * 2**20
        ),
    )(activations, out_grad, accum, noise)


def solution(mesh):
    in_specs = (
        P("dp", "tensor"),
        P(("dp", "tensor"), None),
        P(("tensor", "dp"), None),
        P(("tensor", "dp"), None),
    )
    out_specs = (P(("tensor", "dp"), None), P("dp"))
    return jax.shard_map(local, mesh=mesh, in_specs=in_specs, out_specs=out_specs, check_vma=False)
```

```python
import functools
import math

import jax
import jax.numpy as jnp
from jax import lax
from jax.experimental import pallas as pl
from jax.experimental.pallas import tpu as pltpu
from jax.sharding import PartitionSpec as P

MESH = pl.DeviceIdType.MESH
LEN = 512
FF = 2304
D = 2304
HALF = D // 2
ROWS = 64
SUB = 16
NSUB = ROWS // SUB
CHUNK = 144
WIDTH = (640, 512)
START = (0, 640)
STEP = 48
TOP = 80

SLOT = ((0, 1, 3, 5, 7), (0, 2, 4, 6, 7))
SUBS = ((0, 1, 2, 3), (2, 3, 0, 1))
BLOCK = (0, -1, 1, -2, 2, -3, 3, 4)
GATHER = 3 * NSUB + NSUB // 2

ORDER = ((2, 3, 1, 0, 2, 3), (1, 0, 2, 3, 1, 0))

POWER = 9
REACH = 2.0**14


def encode(x, scale):
    y = x * scale
    y2 = y * y
    y4 = y2 * y2
    return (y4 * y4 * y).astype(jnp.bfloat16)


def decode(sent, unscale):
    z = sent.astype(jnp.float32)
    r = jnp.exp(jnp.log(jnp.abs(z)) * (1.0 / POWER)) * unscale
    return jnp.where(z < 0, -r, r)


def fold(prod):
    total = None
    for i in range(0, prod.shape[0], 8):
        for j in range(0, prod.shape[1], 128):
            piece = prod[i : i + 8, j : j + 128]
            total = piece if total is None else total + piece
    return total


def kernel(
    bound, h_hbm, g_hbm, acc_hbm, noise_hbm, out_ref, clip_ref,
    hs, hp, ht, gs, gp, t, gram, norm, norms, send0, send1, recv0, recv1, last0, last1, sum0, sum1,
    swap0, swap1, fin, acc, noise,
    load_sem, gs_send, gs_recv, hp_send, hp_recv, gp_send, gp_recv, n_send, n_recv, rs_send, rs_recv, last_send, last_recv,
    swap_send, swap_recv,
):
    dp, z = lax.axis_index("dp"), lax.axis_index("tensor")
    x, y, c = dp // 8, (dp // 2) % 4, dp % 2
    o = 1 - c
    partner = (dp - c + o, z)
    along_z = ((dp, (z + 1) % 8), (dp, (z + 7) % 8))
    sends, recvs, sums = (send0, send1), (recv0, recv1), (sum0, sum1)
    lasts, swaps = (last0, last1), (swap0, swap1)

    ia = (x * o + y * c, y * o + x * c)
    ib = (ia[1], ia[0])
    step_a = (4 * o + c, o + 4 * c)
    step_b = (step_a[1], step_a[0])

    def chunk_of(part, a, b):
        return ((ia[part] + a + 4) % 4) * step_a[part] + ((ib[part] + b + 4) % 4) * step_b[part]

    def device_of(part, a, b):
        return (chunk_of(part, a, b) * 2 + c, z)

    loads = []
    for s in range(8):
        row = pl.multiple_of(((z + BLOCK[s] + 8) % 8) * ROWS, ROWS)
        loads.append(pltpu.make_async_copy(h_hbm.at[pl.ds(row, ROWS)], hs.at[pl.ds(s * ROWS, ROWS)], load_sem.at[s]))
    g_load = pltpu.make_async_copy(g_hbm, gs.at[pl.ds(0, ROWS)], load_sem.at[8])
    acc_load = pltpu.make_async_copy(acc_hbm, acc, load_sem.at[9])
    noise_load = pltpu.make_async_copy(noise_hbm, noise, load_sem.at[10])
    g_load.start()
    for copy in loads:
        copy.start()
    acc_load.start()
    noise_load.start()

    others = [*along_z, partner]
    for a, b in ((1, 0), (-1, 0), (0, 1), (0, -1)):
        others += [device_of(0, a, b), (chunk_of(0, a, b) * 2 + o, z)]
    barrier = pltpu.get_barrier_semaphore()
    for device in others:
        pl.semaphore_signal(barrier, inc=1, device_id=device, device_id_type=MESH)
    pl.semaphore_wait(barrier, len(others))

    def gather(way, n):
        sub = SUBS[way][n % NSUB]
        src = gs.at[pl.ds(SLOT[way][n // NSUB] * ROWS + sub * SUB, SUB)]
        dst = gs.at[pl.ds(SLOT[way][n // NSUB + 1] * ROWS + sub * SUB, SUB)]
        return pltpu.make_async_remote_copy(
            src_ref=src, dst_ref=dst, send_sem=gs_send.at[way, n], recv_sem=gs_recv.at[way, n],
            device_id=along_z[way], device_id_type=MESH,
        )

    def give_h(s):
        return pltpu.make_async_remote_copy(
            src_ref=hs.at[pl.ds(s * ROWS, ROWS)], dst_ref=hp.at[pl.ds(s * ROWS, ROWS)],
            send_sem=hp_send.at[s], recv_sem=hp_recv.at[s], device_id=partner, device_id_type=MESH,
        )

    mine = pl.ds(pl.multiple_of(c * HALF, 128), HALF)
    theirs = pl.ds(pl.multiple_of(o * HALF, 128), HALF)

    def give_g(s):
        return pltpu.make_async_remote_copy(
            src_ref=gs.at[pl.ds(s * ROWS, ROWS), theirs], dst_ref=gp.at[pl.ds(s * ROWS, ROWS)],
            send_sem=gp_send.at[s], recv_sem=gp_recv.at[s], device_id=partner, device_id_type=MESH,
        )

    g_load.wait()
    for n in range(NSUB):
        for way in range(2):
            gather(way, n).start()
    give_g(0).start()
    for s in range(8):
        loads[s].wait()
        give_h(s).start()

    def act_gram(i, _):
        r = pl.ds(pl.multiple_of(i * 128, 128), 128)
        gram[r, :] = lax.dot_general(
            hs[r, :], hs[...], (((1,), (1,)), ((), ())), preferred_element_type=jnp.float32
        )
        return 0

    def transpose(src, e):
        def body(i, _):
            r = pl.ds(pl.multiple_of(i * 128, 128), 128)
            ht[e, r, :] = src[:, r].T
            return 0

        lax.fori_loop(0, FF // 128, body, 0)

    def out_gram(lo, hi):
        prod = gram[lo:hi, 0:hi] * lax.dot_general(
            gs[lo:hi, :], gs[0:hi, :], (((1,), (1,)), ((), ())), preferred_element_type=jnp.float32
        )
        total = fold(prod[:, lo:hi])
        return total if lo == 0 else total + 2.0 * fold(prod[:, 0:lo])

    def terms(e):
        def body(i, _):
            r = pl.ds(pl.multiple_of(i * 256, 256), 256)
            rhs = gs[0:256, mine] if e == 0 else gp[0:256, :]
            t[e, r, :] = jnp.dot(ht[e, r, 0:256], rhs, preferred_element_type=jnp.float32)
            return 0

        lax.fori_loop(0, FF // 256, body, 0)

    for n in range(GATHER):
        for way in range(2):
            gather(way, n).wait_recv()
            if n + NSUB < GATHER:
                gather(way, n + NSUB).start()
        if n % NSUB == NSUB - 1:
            for way in range(2):
                give_g(SLOT[way][n // NSUB + 1]).start()
        if n == 0:
            lax.fori_loop(0, 4, act_gram, 0)
        elif n == 1:
            transpose(hs, 0)
        elif n == 3:
            for s in range(8):
                give_h(s).wait_recv()
            transpose(hp, 1)
        elif n == 8:
            norm[...] = out_gram(0, 256)
            terms(0)
        elif n == 9:
            for s in range(4):
                give_g(s).wait_recv()
            terms(1)
        elif n == 11:
            norm[...] += out_gram(256, 384)
    give_g(7).start()

    norm[...] += out_gram(384, 512)

    def give_norm(e, k):
        device = (dp if e == 0 else partner[0], (z + k) % 8)
        return pltpu.make_async_remote_copy(
            src_ref=norm, dst_ref=norms.at[e, k], send_sem=n_send.at[e, k], recv_sem=n_recv.at[e, k],
            device_id=device, device_id_type=MESH,
        )

    pairs = [(e, k) for k in (4, 3, 5, 2, 6, 1, 7, 0) for e in range(2) if (e, k) != (0, 0)]
    for e, k in pairs:
        give_norm(e, k).start()
    for s in range(4, 8):
        give_g(s).wait_recv()

    def finish(part, a, b):
        rows = pl.ds(pl.multiple_of(chunk_of(part, a, b) * CHUNK, 16), CHUNK)
        cols = slice(START[part], START[part] + WIDTH[part])
        for e in range(2):
            if e == 0:
                rhs = gs[256:512, pl.ds(pl.multiple_of(c * HALF + START[part], 128), WIDTH[part])]
            else:
                rhs = gp[256:512, cols]
            t[e, rows, cols] += jnp.dot(ht[e, rows, 256:512], rhs, preferred_element_type=jnp.float32)

    for part in range(2):
        for way in range(2):
            finish(part, 2, ORDER[way][0])
    for e, k in pairs:
        give_norm(e, k).wait_recv()

    def factor(e):
        total = norm[...] if e == 0 else norms[1, 0]
        for k in range(1, 8):
            total = total + norms[e, k]
        sq_norm = jnp.broadcast_to(jnp.sum(total), (8, 128))
        return jnp.max(jnp.minimum(1.0, bound / jnp.sqrt(sq_norm)))

    f0, f1 = factor(0), factor(1)
    clip_ref[0] = f0

    limit = 2.0 * bound
    scale = [REACH / (limit * chips) for chips in (1, 1, 1, 1, 2, 2, 4, 8)]

    def own(part, chunk, r):
        rows = pl.ds(pl.multiple_of(chunk * CHUNK + r, 16), STEP)
        cols = slice(START[part], START[part] + WIDTH[part])
        return f0 * t[0, rows, cols] + f1 * t[1, rows, cols]

    def over_rows(body):
        def step(i, _):
            r = pl.multiple_of(i * STEP, 16)
            body(r, pl.ds(r, STEP))
            return 0

        lax.fori_loop(0, CHUNK // STEP, step, 0)

    def message(part, way, slot):
        sign = 1 - 2 * way
        rows = pl.ds(0, CHUNK)
        if slot == 6:
            rows = pl.ds(0, TOP) if way == 0 else pl.ds(TOP, CHUNK - TOP)
        device = device_of(part, sign, 0) if slot < 6 else device_of(part, 0, sign)
        return pltpu.make_async_remote_copy(
            src_ref=sends[part].at[way, slot, rows], dst_ref=recvs[part].at[way, slot, rows],
            send_sem=rs_send.at[part, way, slot], recv_sem=rs_recv.at[part, way, slot],
            device_id=device, device_id_type=MESH,
        )

    def first_phase(part, way, slot):
        a, b = 2 if slot < 2 else 1 - 2 * way, ORDER[way][slot]
        if slot > 0:
            finish(part, a, b)
        if slot >= 4:
            message(part, way, slot - 4).wait_recv()

        def body(r, rows):
            value = own(part, chunk_of(part, a, b), r)
            if slot >= 4:
                value += decode(recvs[part][way, slot - 4, rows, :], 1.0 / scale[slot - 4])
            sends[part][way, slot, rows, :] = encode(value, scale[slot])

        over_rows(body)
        message(part, way, slot).start()

    def own_sum(part, b):
        finish(part, 0, b)

        def body(r, rows):
            sums[part][b, rows, :] = own(part, chunk_of(part, 0, b), r)

        over_rows(body)

    def take(part, way, slot):
        message(part, way, slot).wait_recv()

        def body(r, rows):
            sums[part][ORDER[way][slot], rows, :] += decode(recvs[part][way, slot, rows, :], 1.0 / scale[slot])

        over_rows(body)

    def both(step, slots):
        for way in range(2):
            for part in range(2):
                step(part, way, slots[way])

    both(first_phase, (0, 0))
    both(first_phase, (2, 2))
    for b in (2, 1):
        for part in range(2):
            own_sum(part, b)
    both(first_phase, (4, 4))
    both(first_phase, (1, 1))
    for b in (3, 0):
        for part in range(2):
            own_sum(part, b)

    for way in range(2):
        for n in range(GATHER):
            gather(way, n).wait_send()
    for s in range(8):
        give_h(s).wait_send()
        give_g(s).wait_send()
    for e, k in pairs:
        give_norm(e, k).wait_send()

    both(take, (2, 2))
    both(take, (4, 4))

    for part in range(2):

        def body(r, rows):
            value = encode(sums[part][2, rows, :], scale[6])
            for way in range(2):
                sends[part][way, 6, rows, :] = value

        over_rows(body)
        for way in range(2):
            message(part, way, 6).start()

    both(first_phase, (5, 3))
    both(first_phase, (3, 5))

    def window(core):
        return pl.ds(pl.multiple_of(core * (CHUNK - TOP), 16), TOP)

    def last(part, way, which):
        core = c if which == 0 else o
        return pltpu.make_async_remote_copy(
            src_ref=sends[part].at[way, 7, window(core)], dst_ref=lasts[part].at[which, way],
            send_sem=last_send.at[part, way, which], recv_sem=last_recv.at[part, way, which],
            device_id=(chunk_of(part, 0, 1 - 2 * way) * 2 + core, z), device_id_type=MESH,
        )

    def pass_on(part, way):
        b = 1 if way == 0 else 3
        rows = slice(0, TOP) if way == 0 else slice(TOP, CHUNK)
        message(part, way, 6).wait_recv()
        sums[part][b, rows, :] += decode(recvs[part][way, 6, rows, :], 1.0 / scale[6])

        def body(r, rows):
            sends[part][way, 7, rows, :] = encode(sums[part][b, rows, :], scale[7])

        over_rows(body)
        for which in range(2):
            last(part, way, which).start()

    for part in range(2):
        pass_on(part, 0)
    both(take, (5, 3))
    for part in range(2):
        pass_on(part, 1)
    both(take, (3, 5))

    def swap(part):
        return pltpu.make_async_remote_copy(
            src_ref=sums[part].at[0, window(o)], dst_ref=swaps[part],
            send_sem=swap_send.at[part], recv_sem=swap_recv.at[part], device_id=partner, device_id_type=MESH,
        )

    for part in range(2):
        swap(part).start()
    acc_load.wait()
    noise_load.wait()
    out_ref[...] = acc[...] + noise[...]
    for part in range(2):
        swap(part).wait_recv()
        for way in range(2):
            for slot in range(7):
                message(part, way, slot).wait_send()

    for part in range(2):
        cols = slice(START[part], START[part] + WIDTH[part])
        for which in range(2):
            for way in range(2):
                last(part, way, which).wait_recv()
            value = sums[part][0, window(c), :] if which == 0 else swaps[part][...]
            for way in range(2):
                value += decode(lasts[part][which, way], 1.0 / scale[7])
            fin[which, :, cols] = value
    kept = pl.ds(pl.multiple_of(c * 8, 8), CHUNK // 2)
    out_ref[:, mine] += fin[0, kept, :]
    out_ref[:, theirs] += fin[1, kept, :]

    for part in range(2):
        swap(part).wait_send()
        for way in range(2):
            for which in range(2):
                last(part, way, which).wait_send()


def local(activations, out_grad, accum, noise):
    hidden_all = activations.shape[1] * lax.axis_size("tensor")
    bound = 0.02 * math.sqrt(activations.shape[0] * hidden_all * out_grad.shape[1])
    f32, bf16, dma = jnp.float32, jnp.bfloat16, pltpu.SemaphoreType.DMA
    hbm = pl.BlockSpec(memory_space=pl.ANY)
    return pl.pallas_call(
        functools.partial(kernel, bound),
        out_shape=(jax.ShapeDtypeStruct(accum.shape, f32), jax.ShapeDtypeStruct((1,), f32)),
        in_specs=[hbm] * 4,
        out_specs=(pl.BlockSpec(memory_space=pltpu.VMEM), pl.BlockSpec(memory_space=pltpu.SMEM)),
        scratch_shapes=[
            pltpu.VMEM((LEN, FF), bf16),
            pltpu.VMEM((LEN, FF), bf16),
            pltpu.VMEM((2, FF, LEN), bf16),
            pltpu.VMEM((LEN, D), bf16),
            pltpu.VMEM((LEN, HALF), bf16),
            pltpu.VMEM((2, FF, HALF), f32),
            pltpu.VMEM((LEN, LEN), f32),
            pltpu.VMEM((8, 128), f32),
            pltpu.VMEM((2, 8, 8, 128), f32),
            pltpu.VMEM((2, 8, CHUNK, WIDTH[0]), bf16),
            pltpu.VMEM((2, 8, CHUNK, WIDTH[1]), bf16),
            pltpu.VMEM((2, 8, CHUNK, WIDTH[0]), bf16),
            pltpu.VMEM((2, 8, CHUNK, WIDTH[1]), bf16),
            pltpu.VMEM((2, 2, TOP, WIDTH[0]), bf16),
            pltpu.VMEM((2, 2, TOP, WIDTH[1]), bf16),
            pltpu.VMEM((4, CHUNK, WIDTH[0]), f32),
            pltpu.VMEM((4, CHUNK, WIDTH[1]), f32),
            pltpu.VMEM((TOP, WIDTH[0]), f32),
            pltpu.VMEM((TOP, WIDTH[1]), f32),
            pltpu.VMEM((2, TOP, HALF), f32),
            pltpu.VMEM(accum.shape, f32),
            pltpu.VMEM(accum.shape, f32),
            dma((11,)),
            dma((2, GATHER)),
            dma((2, GATHER)),
            dma((8,)),
            dma((8,)),
            dma((8,)),
            dma((8,)),
            dma((2, 8)),
            dma((2, 8)),
            dma((2, 2, 8)),
            dma((2, 2, 8)),
            dma((2, 2, 2)),
            dma((2, 2, 2)),
            dma((2,)),
            dma((2,)),
        ],
        compiler_params=pltpu.CompilerParams(
            collective_id=0, has_side_effects=True, vmem_limit_bytes=62 * 2**20
        ),
    )(activations, out_grad, accum, noise)


def solution(mesh):
    in_specs = (
        P("dp", "tensor"),
        P(("dp", "tensor"), None),
        P(("tensor", "dp"), None),
        P(("tensor", "dp"), None),
    )
    out_specs = (P(("tensor", "dp"), None), P("dp"))
    return jax.shard_map(local, mesh=mesh, in_specs=in_specs, out_specs=out_specs, check_vma=False)
```

```python
import functools
import math

import jax
import jax.numpy as jnp
from jax import lax
from jax.experimental import pallas as pl
from jax.experimental.pallas import tpu as pltpu
from jax.sharding import PartitionSpec as P

MESH = pl.DeviceIdType.MESH
LEN = 512
FF = 2304
D = 2304
HALF = D // 2
ROWS = 64
SUB = 16
NSUB = ROWS // SUB
CHUNK = 144
WIDTH = (640, 512)
START = (0, 640)
STEP = 48
TOP = 80

PHASE_START = (0, 512, 896)
PHASE_WIDTH = (512, 384, 256)
PIECE_WIDTH = ((256, 256, 128), (256, 128, 128))
PIECE_START = ((0, 256, 512), (0, 256, 384))

SLOT = ((0, 1, 3, 5, 7), (0, 2, 4, 6, 7))
SUBS = ((0, 1, 2, 3), (2, 3, 0, 1))
BLOCK = (0, -1, 1, -2, 2, -3, 3, 4)
GATHER = 14
SEQUENCE = (
    (0, 1), (2, 3), (0, 0), (0, 2), (0, 3), (1, 0), (2, 0), (0, 5), (2, 1), (1, 3), (0, 4),
    (1, 2), (0, 7), (1, 1), (0, 9), (0, 6), (0, 8), (1, 4), (0, 11), (1, 5), (0, 13), (0, 10),
    (2, 2), (0, 12), (2, 4), (2, 5), (1, 6), (1, 8), (1, 9), (1, 7), (2, 7), (2, 6), (2, 8),
    (2, 9), (1, 10), (1, 12), (1, 13), (1, 11), (2, 11), (2, 10), (2, 12), (2, 13),
)
SPARE = (0.6, 0.45, 0.3)
GROUPS = ((0, 64), (64, 192), (192, 320), (320, 448), (448, 512))

ORDER = ((1, 0, 2, 3), (2, 3, 1, 0))
AHEAD = ((2, 3), (1, 0))

POWER = 9
REACH = 2.0**14
AHEAD_SCALE = 0.9


def encode(x, scale):
    y = x * scale
    y2 = y * y
    y4 = y2 * y2
    return (y4 * y4 * y).astype(jnp.bfloat16)


def decode(sent, unscale):
    z = sent.astype(jnp.float32)
    r = jnp.exp(jnp.log(jnp.abs(z)) * (1.0 / POWER)) * unscale
    return jnp.where(z < 0, -r, r)


def fold(prod):
    total = None
    for i in range(0, prod.shape[0], 8):
        for j in range(0, prod.shape[1], 128):
            piece = prod[i : i + 8, j : j + 128]
            total = piece if total is None else total + piece
    return total


def kernel(
    bound, h_hbm, g_hbm, acc_hbm, noise_hbm, out_ref, clip_ref,
    hs, hp, ht, gs0, gs1, gs2, gp0, gp1, gp2, t, gram, norm, norms, factors, others_factors,
    as00, as01, as02, as10, as11, as12, ar00, ar01, ar02, ar10, ar11, ar12,
    send0, send1, recv0, recv1, last0, last1, sum0, sum1, swap0, swap1, fin, acc, noise,
    load_sem, gs_send, gs_recv, hp_send, hp_recv, gp_send, gp_recv, n_send, n_recv, f_send, f_recv, a_send, a_recv,
    rs_send, rs_recv, last_send, last_recv, swap_send, swap_recv,
):
    gs, gp = (gs0, gs1, gs2), (gp0, gp1, gp2)
    asend, arecv = ((as00, as01, as02), (as10, as11, as12)), ((ar00, ar01, ar02), (ar10, ar11, ar12))
    dp, z = lax.axis_index("dp"), lax.axis_index("tensor")
    x, y, c = dp // 8, (dp // 2) % 4, dp % 2
    o = 1 - c
    partner = (dp - c + o, z)
    along_z = ((dp, (z + 1) % 8), (dp, (z + 7) % 8))
    sends, recvs, sums = (send0, send1), (recv0, recv1), (sum0, sum1)
    lasts, swaps = (last0, last1), (swap0, swap1)

    ia = (x * o + y * c, y * o + x * c)
    ib = (ia[1], ia[0])
    step_a = (4 * o + c, o + 4 * c)
    step_b = (step_a[1], step_a[0])

    def chunk_of(part, a, b):
        return ((ia[part] + a + 4) % 4) * step_a[part] + ((ib[part] + b + 4) % 4) * step_b[part]

    def device_of(part, a, b):
        return (chunk_of(part, a, b) * 2 + c, z)

    loads = []
    for s in range(8):
        row = pl.multiple_of(((z + BLOCK[s] + 8) % 8) * ROWS, ROWS)
        loads.append(pltpu.make_async_copy(h_hbm.at[pl.ds(row, ROWS)], hs.at[pl.ds(s * ROWS, ROWS)], load_sem.at[s]))
    g_loads = []
    for j in range(3):
        for half in range(2):
            src = g_hbm.at[:, pl.ds(half * HALF + PHASE_START[j], PHASE_WIDTH[j])]
            dst = gs[j].at[pl.ds(0, ROWS), pl.ds(half * PHASE_WIDTH[j], PHASE_WIDTH[j])]
            g_loads.append(pltpu.make_async_copy(src, dst, load_sem.at[8 + 2 * j + half]))
    acc_load = pltpu.make_async_copy(acc_hbm, acc, load_sem.at[14])
    noise_load = pltpu.make_async_copy(noise_hbm, noise, load_sem.at[15])
    for copy in g_loads:
        copy.start()
    for copy in loads:
        copy.start()
    acc_load.start()
    noise_load.start()

    others = [*along_z, partner]
    for a, b in ((1, 0), (-1, 0), (0, 1), (0, -1)):
        others += [device_of(0, a, b), (chunk_of(0, a, b) * 2 + o, z)]
    barrier = pltpu.get_barrier_semaphore()
    for device in others:
        pl.semaphore_signal(barrier, inc=1, device_id=device, device_id_type=MESH)
    pl.semaphore_wait(barrier, len(others))

    def gather(j, way, n):
        sub = SUBS[way][n % NSUB]
        src = gs[j].at[pl.ds(SLOT[way][n // NSUB] * ROWS + sub * SUB, SUB)]
        dst = gs[j].at[pl.ds(SLOT[way][n // NSUB + 1] * ROWS + sub * SUB, SUB)]
        return pltpu.make_async_remote_copy(
            src_ref=src, dst_ref=dst, send_sem=gs_send.at[j, way, n], recv_sem=gs_recv.at[j, way, n],
            device_id=along_z[way], device_id_type=MESH,
        )

    def give_h(s):
        return pltpu.make_async_remote_copy(
            src_ref=hs.at[pl.ds(s * ROWS, ROWS)], dst_ref=hp.at[pl.ds(s * ROWS, ROWS)],
            send_sem=hp_send.at[s], recv_sem=hp_recv.at[s], device_id=partner, device_id_type=MESH,
        )

    def give_g(j, group):
        lo, hi = GROUPS[group]
        cols = pl.ds(pl.multiple_of(o * PHASE_WIDTH[j], 128), PHASE_WIDTH[j])
        return pltpu.make_async_remote_copy(
            src_ref=gs[j].at[pl.ds(lo, hi - lo), cols], dst_ref=gp[j].at[pl.ds(lo, hi - lo)],
            send_sem=gp_send.at[j, group], recv_sem=gp_recv.at[j, group], device_id=partner, device_id_type=MESH,
        )

    def act_gram(i, _):
        r = pl.ds(pl.multiple_of(i * 128, 128), 128)
        gram[r, :] = lax.dot_general(
            hs[r, :], hs[...], (((1,), (1,)), ((), ())), preferred_element_type=jnp.float32
        )
        return 0

    def transpose(src, e, lo, hi):
        def body(i, _):
            r = pl.ds(pl.multiple_of(i * 128, 128), 128)
            ht[e, r, :] = src[:, r].T
            return 0

        lax.fori_loop(lo, hi, body, 0)

    def out_gram(j, lo, hi):
        prod = gram[lo:hi, 0:hi] * lax.dot_general(
            gs[j][lo:hi, :], gs[j][0:hi, :], (((1,), (1,)), ((), ())), preferred_element_type=jnp.float32
        )
        total = fold(prod[:, lo:hi])
        if lo > 0:
            total += 2.0 * fold(prod[:, 0:lo])
        if j == 0 and lo == 0:
            norm[...] = total
        else:
            norm[...] += total

    def term(e, part, j, chunk):
        rows = pl.ds(pl.multiple_of(chunk * CHUNK, 16), CHUNK)
        skip = 0 if part == 0 else PIECE_WIDTH[0][j]
        if e == 0:
            cols = pl.ds(pl.multiple_of(c * PHASE_WIDTH[j] + skip, 128), PIECE_WIDTH[part][j])
            rhs = gs[j][:, cols]
        else:
            rhs = gp[j][:, skip : skip + PIECE_WIDTH[part][j]]
        return jnp.dot(ht[e, rows, :], rhs, preferred_element_type=jnp.float32)

    def prepare(part, a, b, phases):
        chunk = chunk_of(part, a, b)
        rows = pl.ds(pl.multiple_of(chunk * CHUNK, 16), CHUNK)
        for j in phases:
            start = START[part] + PIECE_START[part][j]
            for e in range(2):
                t[e, rows, start : start + PIECE_WIDTH[part][j]] = term(e, part, j, chunk)

    def ahead(part, way, j):
        return pltpu.make_async_remote_copy(
            src_ref=asend[part][j].at[way], dst_ref=arecv[part][j].at[way],
            send_sem=a_send.at[part, way, j], recv_sem=a_recv.at[part, way, j],
            device_id=device_of(part, 1 - 2 * way, 0), device_id_type=MESH,
        )

    def send_ahead(part, way, j):
        for k in range(2):
            for e in range(2):
                value = term(e, part, j, chunk_of(part, 2, AHEAD[way][k]))
                asend[part][j][way, k, e] = encode(value, AHEAD_SCALE)
        ahead(part, way, j).start()

    for copy in g_loads:
        copy.wait()
    received, sent = set(), 0

    def forward(sent):
        while sent < len(SEQUENCE):
            j, n = SEQUENCE[sent]
            if n >= NSUB and (j, n - NSUB) not in received:
                break
            for way in range(2):
                gather(j, way, n).start()
            sent += 1
        return sent

    sent = forward(sent)
    for j in range(3):
        give_g(j, 0).start()
    for s in range(8):
        loads[s].wait()
        give_h(s).start()

    def wait_h():
        for s in range(8):
            give_h(s).wait_recv()

    def wait_g(j):
        for group in range(5):
            give_g(j, group).wait_recv()

    first = [(part, way) for way in range(2) for part in range(2)]

    work = [(None, 0.3, functools.partial(lax.fori_loop, i, i + 1, act_gram, 0)) for i in range(4)]
    work += [(None, 0.4, functools.partial(transpose, hs, 0, i, i + 3)) for i in range(0, 18, 3)]
    work += [(None, 0.1, functools.partial(wait_h))]
    work += [(None, 0.4, functools.partial(transpose, hp, 1, i, i + 3)) for i in range(0, 18, 3)]
    later = []
    for j in range(3):
        here = (j, GATHER)
        terms_of = [(here, 0.1, functools.partial(wait_g, j))]
        terms_of += [(here, 0.5 - 0.1 * j, functools.partial(send_ahead, part, way, j)) for part, way in first]
        work += [
            ((j, need), 0.2, functools.partial(out_gram, j, lo, hi))
            for need, lo, hi in ((8, 0, 256), (12, 256, 384), (14, 384, 512))
        ]
        ready = [
            (here, 0.2, functools.partial(prepare, part, 1 - 2 * way, ORDER[way][0], (j,))) for part, way in first
        ]
        if j < 2:
            work += terms_of
            later += ready
        else:
            work += later
            late = terms_of[:1] + ready
            late += [
                (here, 0.2, functools.partial(prepare, part, 2, b, (j,))) for part, way in first for b in AHEAD[way]
            ]

    spare, steps, whole, taken = 0.0, 0, {}, set()
    for j, n in SEQUENCE:
        for way in range(2):
            gather(j, way, n).wait_recv()
        received.add((j, n))
        sent = forward(sent)
        d = n // NSUB
        if {(j, k) for k in range(d * NSUB, min(d * NSUB + NSUB, GATHER))} <= received:
            give_g(j, d + 1).start()
        spare = SPARE[j] + min(spare, 0.3)
        steps += 1
        for phase in range(3):
            if phase not in whole and {(phase, k) for k in range(GATHER)} <= received:
                whole[phase] = steps
        for entry in list(work):
            gate, cost, item = entry
            if item.func is wait_g:
                ready = steps >= whole.get(gate[0], steps) + 2
            else:
                ready = gate is None or {(gate[0], k) for k in range(gate[1])} <= received
                ready = ready and not (item.func in (send_ahead, prepare) and gate[0] not in taken)
            if ready and spare >= cost:
                item()
                spare -= cost
                work.remove(entry)
                if item.func is wait_g:
                    taken.add(gate[0])

    late = [entry for entry in work if entry[2].func is not out_gram] + late
    for _, _, item in work:
        if item.func is out_gram:
            item()

    def give_norm(e, k):
        device = (dp if e == 0 else partner[0], (z + k) % 8)
        return pltpu.make_async_remote_copy(
            src_ref=norm, dst_ref=norms.at[e, k], send_sem=n_send.at[e, k], recv_sem=n_recv.at[e, k],
            device_id=device, device_id_type=MESH,
        )

    pairs = [(e, k) for k in (4, 3, 5, 2, 6, 1, 7, 0) for e in range(2) if (e, k) != (0, 0)]
    for e, k in pairs:
        give_norm(e, k).start()
    for _, _, item in late:
        item()
    for e, k in pairs:
        give_norm(e, k).wait_recv()

    def factor(e):
        total = norm[...] if e == 0 else norms[1, 0]
        for k in range(1, 8):
            total = total + norms[e, k]
        sq_norm = jnp.broadcast_to(jnp.sum(total), (8, 128))
        factors[e] = jnp.minimum(1.0, bound / jnp.sqrt(sq_norm))
        return jnp.max(factors[e])

    f0, f1 = factor(0), factor(1)
    clip_ref[0] = f0

    def give_factors(part, way):
        return pltpu.make_async_remote_copy(
            src_ref=factors, dst_ref=others_factors.at[part, way], send_sem=f_send.at[part, way],
            recv_sem=f_recv.at[part, way], device_id=device_of(part, 1 - 2 * way, 0), device_id_type=MESH,
        )


    limit = 2.0 * bound
    scale = [REACH / (limit * chips) for chips in (1, 1, 2, 2, 4, 8)]

    def own(part, chunk, r):
        rows = pl.ds(pl.multiple_of(chunk * CHUNK + r, 16), STEP)
        cols = slice(START[part], START[part] + WIDTH[part])
        return f0 * t[0, rows, cols] + f1 * t[1, rows, cols]

    def over_rows(body):
        def step(i, _):
            r = pl.multiple_of(i * STEP, 16)
            body(r, pl.ds(r, STEP))
            return 0

        lax.fori_loop(0, CHUNK // STEP, step, 0)

    def send_last_phase(part, way):
        cols = slice(START[part] + PIECE_START[part][2], START[part] + WIDTH[part])
        for k in range(2):
            chunk = chunk_of(part, 2, AHEAD[way][k])

            def body(r, rows):
                mine = pl.ds(pl.multiple_of(chunk * CHUNK + r, 16), STEP)
                value = f0 * t[0, mine, cols] + f1 * t[1, mine, cols]
                asend[part][2][way, k, 0, rows, :] = encode(value, scale[0])

            over_rows(body)
        ahead(part, way, 2).start()

    for part in range(2):
        for way in range(2):
            give_factors(part, way).start()
            send_last_phase(part, way)

    def message(part, way, slot):
        sign = 1 - 2 * way
        rows = pl.ds(0, CHUNK)
        if slot == 4:
            rows = pl.ds(0, TOP) if way == 0 else pl.ds(TOP, CHUNK - TOP)
        device = device_of(part, sign, 0) if slot < 4 else device_of(part, 0, sign)
        return pltpu.make_async_remote_copy(
            src_ref=sends[part].at[way, slot, rows], dst_ref=recvs[part].at[way, slot, rows],
            send_sem=rs_send.at[part, way, slot], recv_sem=rs_recv.at[part, way, slot],
            device_id=device, device_id_type=MESH,
        )

    def first_phase(part, way, slot):
        a, b = 1 - 2 * way, ORDER[way][slot]
        if slot > 0:
            prepare(part, a, b, (0, 1, 2))
        if slot == 2:
            give_factors(part, way).wait_recv()
            for j in range(3):
                ahead(part, way, j).wait_recv()
        if slot >= 2:
            their_f = [jnp.max(others_factors[part, way, e]) for e in range(2)]

        def body(r, rows):
            value = own(part, chunk_of(part, a, b), r)
            if slot < 2:
                sends[part][way, slot, rows, :] = encode(value, scale[slot])
                return
            for j in range(3):
                start = PIECE_START[part][j]
                piece = value[:, start : start + PIECE_WIDTH[part][j]]
                if j == 2:
                    piece += decode(arecv[part][j][way, slot - 2, 0, rows, :], 1.0 / scale[0])
                else:
                    for e in range(2):
                        piece += their_f[e] * decode(arecv[part][j][way, slot - 2, e, rows, :], 1.0 / AHEAD_SCALE)
                sends[part][way, slot, rows, start : start + PIECE_WIDTH[part][j]] = encode(piece, scale[slot])

        over_rows(body)
        message(part, way, slot).start()

    def own_sum(part, b):
        prepare(part, 0, b, (0, 1, 2))

        def body(r, rows):
            sums[part][b, rows, :] = own(part, chunk_of(part, 0, b), r)

        over_rows(body)

    def take(part, way, slot):
        message(part, way, slot).wait_recv()

        def body(r, rows):
            sums[part][ORDER[way][slot], rows, :] += decode(recvs[part][way, slot, rows, :], 1.0 / scale[slot])

        over_rows(body)

    def both(step, slots):
        for way in range(2):
            for part in range(2):
                step(part, way, slots[way])

    both(first_phase, (0, 0))
    for b in (2, 1):
        for part in range(2):
            own_sum(part, b)
    both(first_phase, (2, 2))
    both(first_phase, (3, 1))
    for b in (3, 0):
        for part in range(2):
            own_sum(part, b)

    for j in range(3):
        for way in range(2):
            for n in range(GATHER):
                gather(j, way, n).wait_send()
            for part in range(2):
                ahead(part, way, j).wait_send()
        for group in range(5):
            give_g(j, group).wait_send()
    for s in range(8):
        give_h(s).wait_send()
    for e, k in pairs:
        give_norm(e, k).wait_send()
    for part in range(2):
        for way in range(2):
            give_factors(part, way).wait_send()

    both(take, (0, 0))
    both(take, (2, 2))

    for part in range(2):

        def body(r, rows):
            value = encode(sums[part][2, rows, :], scale[4])
            for way in range(2):
                sends[part][way, 4, rows, :] = value

        over_rows(body)
        for way in range(2):
            message(part, way, 4).start()

    both(first_phase, (1, 3))

    def window(core):
        return pl.ds(pl.multiple_of(core * (CHUNK - TOP), 16), TOP)

    def last(part, way, which):
        core = c if which == 0 else o
        return pltpu.make_async_remote_copy(
            src_ref=sends[part].at[way, 5, window(core)], dst_ref=lasts[part].at[which, way],
            send_sem=last_send.at[part, way, which], recv_sem=last_recv.at[part, way, which],
            device_id=(chunk_of(part, 0, 1 - 2 * way) * 2 + core, z), device_id_type=MESH,
        )

    def pass_on(part, way):
        b = 1 if way == 0 else 3
        rows = slice(0, TOP) if way == 0 else slice(TOP, CHUNK)
        message(part, way, 4).wait_recv()
        sums[part][b, rows, :] += decode(recvs[part][way, 4, rows, :], 1.0 / scale[4])

        def body(r, rows):
            sends[part][way, 5, rows, :] = encode(sums[part][b, rows, :], scale[5])

        over_rows(body)
        for which in range(2):
            last(part, way, which).start()

    for part in range(2):
        pass_on(part, 0)
    both(take, (3, 1))
    for part in range(2):
        pass_on(part, 1)
    both(take, (1, 3))

    def swap(part):
        return pltpu.make_async_remote_copy(
            src_ref=sums[part].at[0, window(o)], dst_ref=swaps[part],
            send_sem=swap_send.at[part], recv_sem=swap_recv.at[part], device_id=partner, device_id_type=MESH,
        )

    for part in range(2):
        swap(part).start()
    acc_load.wait()
    noise_load.wait()
    out_ref[...] = acc[...] + noise[...]
    for part in range(2):
        swap(part).wait_recv()
        for way in range(2):
            for slot in range(5):
                message(part, way, slot).wait_send()

    for part in range(2):
        cols = slice(START[part], START[part] + WIDTH[part])
        for which in range(2):
            for way in range(2):
                last(part, way, which).wait_recv()
            value = sums[part][0, window(c), :] if which == 0 else swaps[part][...]
            for way in range(2):
                value += decode(lasts[part][which, way], 1.0 / scale[5])
            fin[which, :, cols] = value
    kept = pl.ds(pl.multiple_of(c * 8, 8), CHUNK // 2)
    for which in range(2):
        for part in range(2):
            for j in range(3):
                width = PIECE_WIDTH[part][j]
                skip = PHASE_START[j] + (0 if part == 0 else PIECE_WIDTH[0][j])
                start = START[part] + PIECE_START[part][j]
                cols = pl.ds(pl.multiple_of((c if which == 0 else o) * HALF + skip, 128), width)
                out_ref[:, cols] += fin[which, kept, start : start + width]

    for part in range(2):
        swap(part).wait_send()
        for way in range(2):
            for which in range(2):
                last(part, way, which).wait_send()


def local(activations, out_grad, accum, noise):
    hidden_all = activations.shape[1] * lax.axis_size("tensor")
    bound = 0.02 * math.sqrt(activations.shape[0] * hidden_all * out_grad.shape[1])
    f32, bf16, dma = jnp.float32, jnp.bfloat16, pltpu.SemaphoreType.DMA
    hbm = pl.BlockSpec(memory_space=pl.ANY)
    return pl.pallas_call(
        functools.partial(kernel, bound),
        out_shape=(jax.ShapeDtypeStruct(accum.shape, f32), jax.ShapeDtypeStruct((1,), f32)),
        in_specs=[hbm] * 4,
        out_specs=(pl.BlockSpec(memory_space=pltpu.VMEM), pl.BlockSpec(memory_space=pltpu.SMEM)),
        scratch_shapes=[
            pltpu.VMEM((LEN, FF), bf16),
            pltpu.VMEM((LEN, FF), bf16),
            pltpu.VMEM((2, FF, LEN), bf16),
            *[pltpu.VMEM((LEN, 2 * width), bf16) for width in PHASE_WIDTH],
            *[pltpu.VMEM((LEN, width), bf16) for width in PHASE_WIDTH],
            pltpu.VMEM((2, FF, HALF), f32),
            pltpu.VMEM((LEN, LEN), f32),
            pltpu.VMEM((8, 128), f32),
            pltpu.VMEM((2, 8, 8, 128), f32),
            pltpu.VMEM((2, 8, 128), f32),
            pltpu.VMEM((2, 2, 2, 8, 128), f32),
            *[pltpu.VMEM((2, 2, 2 - j // 2, CHUNK, part[j]), bf16) for part in PIECE_WIDTH for j in range(3)] * 2,
            pltpu.VMEM((2, 6, CHUNK, WIDTH[0]), bf16),
            pltpu.VMEM((2, 6, CHUNK, WIDTH[1]), bf16),
            pltpu.VMEM((2, 6, CHUNK, WIDTH[0]), bf16),
            pltpu.VMEM((2, 6, CHUNK, WIDTH[1]), bf16),
            pltpu.VMEM((2, 2, TOP, WIDTH[0]), bf16),
            pltpu.VMEM((2, 2, TOP, WIDTH[1]), bf16),
            pltpu.VMEM((4, CHUNK, WIDTH[0]), f32),
            pltpu.VMEM((4, CHUNK, WIDTH[1]), f32),
            pltpu.VMEM((TOP, WIDTH[0]), f32),
            pltpu.VMEM((TOP, WIDTH[1]), f32),
            pltpu.VMEM((2, TOP, HALF), f32),
            pltpu.VMEM(accum.shape, f32),
            pltpu.VMEM(accum.shape, f32),
            dma((16,)),
            dma((3, 2, GATHER)),
            dma((3, 2, GATHER)),
            dma((8,)),
            dma((8,)),
            dma((3, 5)),
            dma((3, 5)),
            dma((2, 8)),
            dma((2, 8)),
            dma((2, 2)),
            dma((2, 2)),
            dma((2, 2, 3)),
            dma((2, 2, 3)),
            dma((2, 2, 5)),
            dma((2, 2, 5)),
            dma((2, 2, 2)),
            dma((2, 2, 2)),
            dma((2,)),
            dma((2,)),
        ],
        compiler_params=pltpu.CompilerParams(
            collective_id=0, has_side_effects=True, vmem_limit_bytes=62 * 2**20
        ),
    )(activations, out_grad, accum, noise)


def solution(mesh):
    in_specs = (
        P("dp", "tensor"),
        P(("dp", "tensor"), None),
        P(("tensor", "dp"), None),
        P(("tensor", "dp"), None),
    )
    out_specs = (P(("tensor", "dp"), None), P("dp"))
    return jax.shard_map(local, mesh=mesh, in_specs=in_specs, out_specs=out_specs, check_vma=False)
```

```python
import functools
import math

import jax
import jax.numpy as jnp
from jax import lax
from jax.experimental import pallas as pl
from jax.experimental.pallas import tpu as pltpu
from jax.sharding import PartitionSpec as P

MESH = pl.DeviceIdType.MESH
LEN = 512
FF = 2304
D = 2304
HALF = D // 2
ROWS = 64
SUB = 16
NSUB = ROWS // SUB
CHUNK = 144
WIDTH = (640, 512)
START = (0, 640)
STEP = 48
TOP = 80

PHASE_START = (0, 512, 896)
PHASE_WIDTH = (512, 384, 256)
PIECE_WIDTH = ((256, 256, 128), (256, 128, 128))
PIECE_START = ((0, 256, 512), (0, 256, 384))

SLOT = ((0, 1, 3, 5, 7), (0, 2, 4, 6, 7))
SUBS = ((0, 1, 2, 3), (2, 3, 0, 1))
BLOCK = (0, -1, 1, -2, 2, -3, 3, 4)
GATHER = 14
SEQUENCE = (
    (0, 1), (2, 3), (0, 0), (0, 2), (0, 3), (1, 0), (2, 0), (0, 5), (2, 1), (1, 3), (0, 4),
    (1, 2), (0, 7), (1, 1), (0, 9), (0, 6), (0, 8), (1, 4), (0, 11), (1, 5), (0, 13), (0, 10),
    (2, 2), (0, 12), (2, 4), (2, 5), (1, 6), (1, 8), (1, 9), (1, 7), (2, 7), (2, 6), (2, 8),
    (2, 9), (1, 10), (1, 12), (1, 13), (1, 11), (2, 11), (2, 10), (2, 12), (2, 13),
)
SPARE = (0.6, 0.45, 0.4)
GROUPS = ((0, 64), (64, 192), (192, 320), (320, 448), (448, 512))

ORDER = ((1, 0, 2, 3), (2, 3, 1, 0))
AHEAD = ((2, 3), (1, 0))

POWER = 9
REACH = 2.0**13.5
LARGEST = 2.0**14.1
TINY = 1e-30
CHIP, TERM = 2, 3


def encode(x, scale):
    y = jnp.clip(x * scale, -LARGEST, LARGEST)
    y2 = y * y
    y4 = y2 * y2
    return (y4 * y4 * y).astype(jnp.bfloat16)


def decode(sent, unscale):
    z = sent.astype(jnp.float32)
    r = jnp.exp(jnp.log(jnp.abs(z)) * (1.0 / POWER)) * unscale
    return jnp.where(z < 0, -r, r)


def fold(prod):
    pieces = [
        prod[i : i + 8, j : j + 128] for i in range(0, prod.shape[0], 8) for j in range(0, prod.shape[1], 128)
    ]
    while len(pieces) > 1:
        pieces = [pieces[i] + pieces[i + 1] if i + 1 < len(pieces) else pieces[i] for i in range(0, len(pieces), 2)]
    return pieces[0]


def kernel(
    bound, h_hbm, g_hbm, acc_hbm, noise_hbm, out_ref, clip_ref,
    hs, hp, ht, gs0, gs1, gs2, gp0, gp1, gp2, t, gram, norm, norms, factors, near, line, far, squares,
    as00, as01, as02, as10, as11, as12, ar00, ar01, ar02, ar10, ar11, ar12,
    send0, send1, recv0, recv1, last0, last1, sum0, sum1, swap0, swap1, fin, acc, noise,
    load_sem, gs_send, gs_recv, hp_send, hp_recv, gp_send, gp_recv, n_send, n_recv, f_send, f_recv, l_send, l_recv, a_send, a_recv,
    rs_send, rs_recv, last_send, last_recv, swap_send, swap_recv,
):
    gs, gp = (gs0, gs1, gs2), (gp0, gp1, gp2)
    asend, arecv = ((as00, as01, as02), (as10, as11, as12)), ((ar00, ar01, ar02), (ar10, ar11, ar12))
    dp, z = lax.axis_index("dp"), lax.axis_index("tensor")
    x, y, c = dp // 8, (dp // 2) % 4, dp % 2
    o = 1 - c
    partner = (dp - c + o, z)
    along_z = ((dp, (z + 1) % 8), (dp, (z + 7) % 8))
    sends, recvs, sums = (send0, send1), (recv0, recv1), (sum0, sum1)
    lasts, swaps = (last0, last1), (swap0, swap1)

    ia = (x * o + y * c, y * o + x * c)
    ib = (ia[1], ia[0])
    step_a = (4 * o + c, o + 4 * c)
    step_b = (step_a[1], step_a[0])

    def chunk_of(part, a, b):
        return ((ia[part] + a + 4) % 4) * step_a[part] + ((ib[part] + b + 4) % 4) * step_b[part]

    def device_of(part, a, b):
        return (chunk_of(part, a, b) * 2 + c, z)

    loads = []
    for s in range(8):
        row = pl.multiple_of(((z + BLOCK[s] + 8) % 8) * ROWS, ROWS)
        loads.append(pltpu.make_async_copy(h_hbm.at[pl.ds(row, ROWS)], hs.at[pl.ds(s * ROWS, ROWS)], load_sem.at[s]))
    g_loads = []
    for j in range(3):
        for half in range(2):
            src = g_hbm.at[:, pl.ds(half * HALF + PHASE_START[j], PHASE_WIDTH[j])]
            dst = gs[j].at[pl.ds(0, ROWS), pl.ds(half * PHASE_WIDTH[j], PHASE_WIDTH[j])]
            g_loads.append(pltpu.make_async_copy(src, dst, load_sem.at[8 + 2 * j + half]))
    acc_load = pltpu.make_async_copy(acc_hbm, acc, load_sem.at[14])
    noise_load = pltpu.make_async_copy(noise_hbm, noise, load_sem.at[15])
    for copy in g_loads:
        copy.start()
    for copy in loads:
        copy.start()
    acc_load.start()
    noise_load.start()

    others = [*along_z, partner]
    for a, b in ((1, 0), (-1, 0), (0, 1), (0, -1)):
        others += [device_of(0, a, b), (chunk_of(0, a, b) * 2 + o, z)]
    barrier = pltpu.get_barrier_semaphore()
    others += [device_of(0, 2, 0), device_of(0, 0, 2)]
    for device in others:
        pl.semaphore_signal(barrier, inc=1, device_id=device, device_id_type=MESH)
    pl.semaphore_wait(barrier, len(others))

    def gather(j, way, n):
        sub = SUBS[way][n % NSUB]
        src = gs[j].at[pl.ds(SLOT[way][n // NSUB] * ROWS + sub * SUB, SUB)]
        dst = gs[j].at[pl.ds(SLOT[way][n // NSUB + 1] * ROWS + sub * SUB, SUB)]
        return pltpu.make_async_remote_copy(
            src_ref=src, dst_ref=dst, send_sem=gs_send.at[j, way, n], recv_sem=gs_recv.at[j, way, n],
            device_id=along_z[way], device_id_type=MESH,
        )

    def give_h(s):
        return pltpu.make_async_remote_copy(
            src_ref=hs.at[pl.ds(s * ROWS, ROWS)], dst_ref=hp.at[pl.ds(s * ROWS, ROWS)],
            send_sem=hp_send.at[s], recv_sem=hp_recv.at[s], device_id=partner, device_id_type=MESH,
        )

    def give_g(j, group):
        lo, hi = GROUPS[group]
        cols = pl.ds(pl.multiple_of(o * PHASE_WIDTH[j], 128), PHASE_WIDTH[j])
        return pltpu.make_async_remote_copy(
            src_ref=gs[j].at[pl.ds(lo, hi - lo), cols], dst_ref=gp[j].at[pl.ds(lo, hi - lo)],
            send_sem=gp_send.at[j, group], recv_sem=gp_recv.at[j, group], device_id=partner, device_id_type=MESH,
        )

    def act_gram(i, _):
        r = pl.ds(pl.multiple_of(i * 128, 128), 128)
        gram[r, :] = lax.dot_general(
            hs[r, :], hs[...], (((1,), (1,)), ((), ())), preferred_element_type=jnp.float32
        )
        return 0

    def transpose(src, e, lo, hi):
        def body(i, _):
            r = pl.ds(pl.multiple_of(i * 128, 128), 128)
            ht[e, r, :] = src[:, r].T
            return 0

        lax.fori_loop(lo, hi, body, 0)

    def out_gram(j, lo, hi):
        prod = gram[lo:hi, 0:hi] * lax.dot_general(
            gs[j][lo:hi, :], gs[j][0:hi, :], (((1,), (1,)), ((), ())), preferred_element_type=jnp.float32
        )
        total = fold(prod[:, lo:hi])
        if lo > 0:
            total += 2.0 * fold(prod[:, 0:lo])
        if j == 0 and lo == 0:
            norm[...] = total
        else:
            norm[...] += total

    def term(e, part, j, chunk):
        rows = pl.ds(pl.multiple_of(chunk * CHUNK, 16), CHUNK)
        skip = 0 if part == 0 else PIECE_WIDTH[0][j]
        if e == 0:
            cols = pl.ds(pl.multiple_of(c * PHASE_WIDTH[j] + skip, 128), PIECE_WIDTH[part][j])
            rhs = gs[j][:, cols]
        else:
            rhs = gp[j][:, skip : skip + PIECE_WIDTH[part][j]]
        return jnp.dot(ht[e, rows, :], rhs, preferred_element_type=jnp.float32)

    def prepare(part, a, b, phases):
        chunk = chunk_of(part, a, b)
        rows = pl.ds(pl.multiple_of(chunk * CHUNK, 16), CHUNK)
        for j in phases:
            start = START[part] + PIECE_START[part][j]
            for e in range(2):
                t[e, rows, start : start + PIECE_WIDTH[part][j]] = term(e, part, j, chunk)

    def ahead(part, way, j):
        return pltpu.make_async_remote_copy(
            src_ref=asend[part][j].at[way], dst_ref=arecv[part][j].at[way],
            send_sem=a_send.at[part, way, j], recv_sem=a_recv.at[part, way, j],
            device_id=device_of(part, 1 - 2 * way, 0), device_id_type=MESH,
        )

    def square(src, e):
        def body(i, total):
            x = src[pl.ds(pl.multiple_of(i * 64, 64), 64), :].astype(jnp.float32)
            return total + fold(x * x)

        total = lax.fori_loop(0, LEN // 64, body, jnp.zeros((8, 128), jnp.float32))
        squares[e] = jnp.sqrt(jnp.broadcast_to(jnp.sum(total), (8, 128)))

    def term_bound(j):
        for e in range(2):
            total = jnp.zeros((8, 128), jnp.float32)
            for r in range(0, LEN, 128):
                if e == 0:
                    x = gs[j][r : r + 128, pl.ds(pl.multiple_of(c * PHASE_WIDTH[j], 128), PHASE_WIDTH[j])]
                else:
                    x = gp[j][r : r + 128, :]
                x = x.astype(jnp.float32)
                total = total + fold(x * x)
            value = squares[e] * jnp.sqrt(jnp.broadcast_to(jnp.sum(total), (8, 128)))
            row = TERM + 2 * j + e
            factors[row : row + 1, :] = jnp.maximum(value, TINY)[0:1]

    def send_ahead(part, way, j):
        for k in range(2):
            for e in range(2):
                value = term(e, part, j, chunk_of(part, 2, AHEAD[way][k]))
                row = TERM + 2 * j + e
                asend[part][j][way, k, e] = encode(value, REACH / factors[row : row + 1, 0:1])
        ahead(part, way, j).start()

    for copy in g_loads:
        copy.wait()
    received, sent = set(), 0

    def forward(sent):
        while sent < len(SEQUENCE):
            j, n = SEQUENCE[sent]
            if n >= NSUB and (j, n - NSUB) not in received:
                break
            for way in range(2):
                gather(j, way, n).start()
            sent += 1
        return sent

    sent = forward(sent)
    for j in range(3):
        give_g(j, 0).start()
    for s in range(8):
        loads[s].wait()
        give_h(s).start()

    def wait_h():
        for s in range(8):
            give_h(s).wait_recv()

    def wait_g(j):
        for group in range(5):
            give_g(j, group).wait_recv()

    first = [(part, way) for way in range(2) for part in range(2)]

    work = [(None, 0.3, functools.partial(lax.fori_loop, i, i + 1, act_gram, 0)) for i in range(4)]
    work += [(None, 0.4, functools.partial(transpose, hs, 0, i, i + 3)) for i in range(0, 18, 3)]
    work += [(None, 0.5, functools.partial(square, hs, 0))]
    work += [(None, 0.1, functools.partial(wait_h))]
    work += [(None, 0.4, functools.partial(transpose, hp, 1, i, i + 3)) for i in range(0, 18, 3)]
    work += [(None, 0.5, functools.partial(square, hp, 1))]
    later = []
    for j in range(3):
        here = (j, GATHER)
        terms_of = [(here, 0.1, functools.partial(wait_g, j))]
        if j < 2:
            terms_of += [(here, 0.2, functools.partial(term_bound, j))]
        terms_of += [(here, 0.5 - 0.1 * j, functools.partial(send_ahead, part, way, j)) for part, way in first]
        work += [
            ((j, need), 0.2, functools.partial(out_gram, j, lo, hi))
            for need, lo, hi in ((8, 0, 256), (12, 256, 384), (14, 384, 512))
        ]
        ready = [
            (here, 0.2, functools.partial(prepare, part, 1 - 2 * way, ORDER[way][0], (j,))) for part, way in first
        ]
        if j < 2:
            work += terms_of
            later += ready
        else:
            work += later
            late = terms_of[:1] + ready
            late += [
                (here, 0.2, functools.partial(prepare, part, 2, b, (j,))) for part, way in first for b in AHEAD[way]
            ]

    spare, steps, whole, taken = 0.0, 0, {}, set()
    for j, n in SEQUENCE:
        for way in range(2):
            gather(j, way, n).wait_recv()
        received.add((j, n))
        sent = forward(sent)
        d = n // NSUB
        if {(j, k) for k in range(d * NSUB, min(d * NSUB + NSUB, GATHER))} <= received:
            give_g(j, d + 1).start()
        spare = SPARE[j] + min(spare, 0.3)
        steps += 1
        for phase in range(3):
            if phase not in whole and {(phase, k) for k in range(GATHER)} <= received:
                whole[phase] = steps
        for entry in list(work):
            gate, cost, item = entry
            if item.func is wait_g:
                ready = steps >= whole.get(gate[0], steps) + 2
            else:
                ready = gate is None or {(gate[0], k) for k in range(gate[1])} <= received
                ready = ready and not (item.func in (term_bound, send_ahead, prepare) and gate[0] not in taken)
            if ready and spare >= cost:
                item()
                spare -= cost
                work.remove(entry)
                if item.func is wait_g:
                    taken.add(gate[0])

    late = [entry for entry in work if entry[2].func is not out_gram] + late
    for _, _, item in work:
        if item.func is out_gram:
            item()

    def give_norm(e, k):
        device = (dp if e == 0 else partner[0], (z + k) % 8)
        return pltpu.make_async_remote_copy(
            src_ref=norm, dst_ref=norms.at[e, k], send_sem=n_send.at[e, k], recv_sem=n_recv.at[e, k],
            device_id=device, device_id_type=MESH,
        )

    pairs = [(e, k) for k in (4, 3, 5, 2, 6, 1, 7, 0) for e in range(2) if (e, k) != (0, 0)]
    for e, k in pairs:
        give_norm(e, k).start()
    for _, _, item in late:
        item()
    for e, k in pairs:
        give_norm(e, k).wait_recv()

    def factor(e):
        total = norm[...] if e == 0 else norms[1, 0]
        for k in range(1, 8):
            total = total + norms[e, k]
        sq_norm = jnp.broadcast_to(jnp.sum(total), (8, 128))
        value = jnp.minimum(1.0, bound / jnp.sqrt(sq_norm))
        return value, value * jnp.sqrt(sq_norm)

    (v0, m0), (v1, m1) = factor(0), factor(1)
    factors[0:1, :] = v0[0:1]
    factors[1:2, :] = v1[0:1]
    factors[CHIP : CHIP + 1, :] = jnp.maximum(m0 + m1, TINY)[0:1]
    f0, f1 = jnp.max(v0), jnp.max(v1)
    clip_ref[0] = f0

    def give_factors(part, k):
        return pltpu.make_async_remote_copy(
            src_ref=factors, dst_ref=near.at[part, k], send_sem=f_send.at[part, k], recv_sem=f_recv.at[part, k],
            device_id=device_of(part, (1, -1, 2)[k], 0), device_id_type=MESH,
        )

    def give_line(part, k):
        return pltpu.make_async_remote_copy(
            src_ref=line.at[part], dst_ref=far.at[part, k], send_sem=l_send.at[part, k], recv_sem=l_recv.at[part, k],
            device_id=device_of(part, 0, (1, -1, 2)[k]), device_id_type=MESH,
        )

    def near_bound(part, k):
        return near[part, k, CHIP : CHIP + 1, 0:1]

    def far_bound(part, k):
        return far[part, k, 0:1, 0:1]

    def sent_bound(part, way, slot):
        if slot < 4:
            own_bound = factors[CHIP : CHIP + 1, 0:1]
            return own_bound if slot < 2 else own_bound + near_bound(part, way)
        own_bound = line[part, 0:1, 0:1]
        return own_bound if slot == 4 else own_bound + far_bound(part, way)

    def got_bound(part, way, slot):
        if slot < 4:
            return near_bound(part, way) if slot < 2 else near_bound(part, way) + near_bound(part, 2)
        return far_bound(part, way) if slot == 4 else far_bound(part, way) + far_bound(part, 2)

    def own(part, chunk, r):
        rows = pl.ds(pl.multiple_of(chunk * CHUNK + r, 16), STEP)
        cols = slice(START[part], START[part] + WIDTH[part])
        return f0 * t[0, rows, cols] + f1 * t[1, rows, cols]

    def over_rows(body):
        def step(i, _):
            r = pl.multiple_of(i * STEP, 16)
            body(r, pl.ds(r, STEP))
            return 0

        lax.fori_loop(0, CHUNK // STEP, step, 0)

    def send_last_phase(part, way):
        scale = REACH / sent_bound(part, way, 0)
        cols = slice(START[part] + PIECE_START[part][2], START[part] + WIDTH[part])
        for k in range(2):
            chunk = chunk_of(part, 2, AHEAD[way][k])

            def body(r, rows):
                mine = pl.ds(pl.multiple_of(chunk * CHUNK + r, 16), STEP)
                value = f0 * t[0, mine, cols] + f1 * t[1, mine, cols]
                asend[part][2][way, k, 0, rows, :] = encode(value, scale)

            over_rows(body)
        ahead(part, way, 2).start()

    for part in range(2):
        for way in range(2):
            send_last_phase(part, way)
    for part in range(2):
        for k in range(3):
            give_factors(part, k).start()

    def message(part, way, slot):
        sign = 1 - 2 * way
        rows = pl.ds(0, CHUNK)
        if slot == 4:
            rows = pl.ds(0, TOP) if way == 0 else pl.ds(TOP, CHUNK - TOP)
        device = device_of(part, sign, 0) if slot < 4 else device_of(part, 0, sign)
        return pltpu.make_async_remote_copy(
            src_ref=sends[part].at[way, slot, rows], dst_ref=recvs[part].at[way, slot, rows],
            send_sem=rs_send.at[part, way, slot], recv_sem=rs_recv.at[part, way, slot],
            device_id=device, device_id_type=MESH,
        )

    def first_phase(part, way, slot):
        a, b = 1 - 2 * way, ORDER[way][slot]
        if slot > 0:
            prepare(part, a, b, (0, 1, 2))
        if slot == 2:
            give_factors(part, way).wait_recv()
            for j in range(3):
                ahead(part, way, j).wait_recv()
        if slot >= 2:
            their_f = [jnp.max(near[part, way, e : e + 1]) for e in range(2)]
            unscale = near[part, way, :, 0:1] * (1.0 / REACH)
        scale = REACH / sent_bound(part, way, slot)

        def body(r, rows):
            value = own(part, chunk_of(part, a, b), r)
            if slot < 2:
                sends[part][way, slot, rows, :] = encode(value, scale)
                return
            for j in range(3):
                start = PIECE_START[part][j]
                piece = value[:, start : start + PIECE_WIDTH[part][j]]
                if j == 2:
                    piece += decode(arecv[part][j][way, slot - 2, 0, rows, :], unscale[CHIP : CHIP + 1])
                else:
                    for e in range(2):
                        row = TERM + 2 * j + e
                        sent = arecv[part][j][way, slot - 2, e, rows, :]
                        piece += decode(sent, unscale[row : row + 1] * their_f[e])
                sends[part][way, slot, rows, start : start + PIECE_WIDTH[part][j]] = encode(piece, scale)

        over_rows(body)
        message(part, way, slot).start()

    def own_sum(part, b):
        prepare(part, 0, b, (0, 1, 2))

        def body(r, rows):
            sums[part][b, rows, :] = own(part, chunk_of(part, 0, b), r)

        over_rows(body)

    def take(part, way, slot):
        message(part, way, slot).wait_recv()
        unscale = got_bound(part, way, slot) * (1.0 / REACH)

        def body(r, rows):
            sums[part][ORDER[way][slot], rows, :] += decode(recvs[part][way, slot, rows, :], unscale)

        over_rows(body)

    def both(step, slots):
        for way in range(2):
            for part in range(2):
                step(part, way, slots[way])

    both(first_phase, (0, 0))
    for b in (2, 1):
        for part in range(2):
            own_sum(part, b)
    both(first_phase, (2, 2))
    for part in range(2):
        give_factors(part, 2).wait_recv()
        total = factors[CHIP : CHIP + 1, :]
        for k in range(3):
            total = total + near[part, k, CHIP : CHIP + 1, :]
        line[part] = jnp.broadcast_to(total, (8, 128))
        for k in range(3):
            give_line(part, k).start()
    both(first_phase, (3, 1))
    for b in (3, 0):
        for part in range(2):
            own_sum(part, b)

    for j in range(3):
        for way in range(2):
            for n in range(GATHER):
                gather(j, way, n).wait_send()
            for part in range(2):
                ahead(part, way, j).wait_send()
        for group in range(5):
            give_g(j, group).wait_send()
    for s in range(8):
        give_h(s).wait_send()
    for e, k in pairs:
        give_norm(e, k).wait_send()
    for part in range(2):
        for k in range(3):
            give_factors(part, k).wait_send()
            give_line(part, k).wait_send()

    both(take, (0, 0))
    both(take, (2, 2))

    for part in range(2):
        scale = REACH / sent_bound(part, 0, 4)

        def body(r, rows):
            value = encode(sums[part][2, rows, :], scale)
            for way in range(2):
                sends[part][way, 4, rows, :] = value

        over_rows(body)
        for way in range(2):
            message(part, way, 4).start()

    both(first_phase, (1, 3))

    def window(core):
        return pl.ds(pl.multiple_of(core * (CHUNK - TOP), 16), TOP)

    def last(part, way, which):
        core = c if which == 0 else o
        return pltpu.make_async_remote_copy(
            src_ref=sends[part].at[way, 5, window(core)], dst_ref=lasts[part].at[which, way],
            send_sem=last_send.at[part, way, which], recv_sem=last_recv.at[part, way, which],
            device_id=(chunk_of(part, 0, 1 - 2 * way) * 2 + core, z), device_id_type=MESH,
        )

    def pass_on(part, way):
        b = 1 if way == 0 else 3
        rows = slice(0, TOP) if way == 0 else slice(TOP, CHUNK)
        message(part, way, 4).wait_recv()
        give_line(part, way).wait_recv()
        sums[part][b, rows, :] += decode(recvs[part][way, 4, rows, :], got_bound(part, way, 4) * (1.0 / REACH))

        scale = REACH / sent_bound(part, way, 5)

        def body(r, rows):
            sends[part][way, 5, rows, :] = encode(sums[part][b, rows, :], scale)

        over_rows(body)
        for which in range(2):
            last(part, way, which).start()

    for part in range(2):
        pass_on(part, 0)
    both(take, (3, 1))
    for part in range(2):
        pass_on(part, 1)
    both(take, (1, 3))

    def swap(part):
        return pltpu.make_async_remote_copy(
            src_ref=sums[part].at[0, window(o)], dst_ref=swaps[part],
            send_sem=swap_send.at[part], recv_sem=swap_recv.at[part], device_id=partner, device_id_type=MESH,
        )

    for part in range(2):
        swap(part).start()
    acc_load.wait()
    noise_load.wait()
    out_ref[...] = acc[...] + noise[...]
    for part in range(2):
        give_line(part, 2).wait_recv()
        swap(part).wait_recv()
        for way in range(2):
            for slot in range(5):
                message(part, way, slot).wait_send()

    for part in range(2):
        cols = slice(START[part], START[part] + WIDTH[part])
        for which in range(2):
            for way in range(2):
                last(part, way, which).wait_recv()
            value = sums[part][0, window(c), :] if which == 0 else swaps[part][...]
            for way in range(2):
                axes = part if which == 0 else 1 - part
                value += decode(lasts[part][which, way], got_bound(axes, way, 5) * (1.0 / REACH))
            fin[which, :, cols] = value
    kept = pl.ds(pl.multiple_of(c * 8, 8), CHUNK // 2)
    for which in range(2):
        for part in range(2):
            for j in range(3):
                width = PIECE_WIDTH[part][j]
                skip = PHASE_START[j] + (0 if part == 0 else PIECE_WIDTH[0][j])
                start = START[part] + PIECE_START[part][j]
                cols = pl.ds(pl.multiple_of((c if which == 0 else o) * HALF + skip, 128), width)
                out_ref[:, cols] += fin[which, kept, start : start + width]

    for part in range(2):
        swap(part).wait_send()
        for way in range(2):
            for which in range(2):
                last(part, way, which).wait_send()


def local(activations, out_grad, accum, noise):
    hidden_all = activations.shape[1] * lax.axis_size("tensor")
    bound = 0.02 * math.sqrt(activations.shape[0] * hidden_all * out_grad.shape[1])
    f32, bf16, dma = jnp.float32, jnp.bfloat16, pltpu.SemaphoreType.DMA
    hbm = pl.BlockSpec(memory_space=pl.ANY)
    return pl.pallas_call(
        functools.partial(kernel, bound),
        out_shape=(jax.ShapeDtypeStruct(accum.shape, f32), jax.ShapeDtypeStruct((1,), f32)),
        in_specs=[hbm] * 4,
        out_specs=(pl.BlockSpec(memory_space=pltpu.VMEM), pl.BlockSpec(memory_space=pltpu.SMEM)),
        scratch_shapes=[
            pltpu.VMEM((LEN, FF), bf16),
            pltpu.VMEM((LEN, FF), bf16),
            pltpu.VMEM((2, FF, LEN), bf16),
            *[pltpu.VMEM((LEN, 2 * width), bf16) for width in PHASE_WIDTH],
            *[pltpu.VMEM((LEN, width), bf16) for width in PHASE_WIDTH],
            pltpu.VMEM((2, FF, HALF), f32),
            pltpu.VMEM((LEN, LEN), f32),
            pltpu.VMEM((8, 128), f32),
            pltpu.VMEM((2, 8, 8, 128), f32),
            pltpu.VMEM((8, 128), f32),
            pltpu.VMEM((2, 3, 8, 128), f32),
            pltpu.VMEM((2, 8, 128), f32),
            pltpu.VMEM((2, 3, 8, 128), f32),
            pltpu.VMEM((2, 8, 128), f32),
            *[pltpu.VMEM((2, 2, 2 - j // 2, CHUNK, part[j]), bf16) for part in PIECE_WIDTH for j in range(3)] * 2,
            pltpu.VMEM((2, 6, CHUNK, WIDTH[0]), bf16),
            pltpu.VMEM((2, 6, CHUNK, WIDTH[1]), bf16),
            pltpu.VMEM((2, 6, CHUNK, WIDTH[0]), bf16),
            pltpu.VMEM((2, 6, CHUNK, WIDTH[1]), bf16),
            pltpu.VMEM((2, 2, TOP, WIDTH[0]), bf16),
            pltpu.VMEM((2, 2, TOP, WIDTH[1]), bf16),
            pltpu.VMEM((4, CHUNK, WIDTH[0]), f32),
            pltpu.VMEM((4, CHUNK, WIDTH[1]), f32),
            pltpu.VMEM((TOP, WIDTH[0]), f32),
            pltpu.VMEM((TOP, WIDTH[1]), f32),
            pltpu.VMEM((2, TOP, HALF), f32),
            pltpu.VMEM(accum.shape, f32),
            pltpu.VMEM(accum.shape, f32),
            dma((16,)),
            dma((3, 2, GATHER)),
            dma((3, 2, GATHER)),
            dma((8,)),
            dma((8,)),
            dma((3, 5)),
            dma((3, 5)),
            dma((2, 8)),
            dma((2, 8)),
            dma((2, 3)),
            dma((2, 3)),
            dma((2, 3)),
            dma((2, 3)),
            dma((2, 2, 3)),
            dma((2, 2, 3)),
            dma((2, 2, 5)),
            dma((2, 2, 5)),
            dma((2, 2, 2)),
            dma((2, 2, 2)),
            dma((2,)),
            dma((2,)),
        ],
        compiler_params=pltpu.CompilerParams(
            collective_id=0, has_side_effects=True, vmem_limit_bytes=62 * 2**20
        ),
    )(activations, out_grad, accum, noise)


def solution(mesh):
    in_specs = (
        P("dp", "tensor"),
        P(("dp", "tensor"), None),
        P(("tensor", "dp"), None),
        P(("tensor", "dp"), None),
    )
    out_specs = (P(("tensor", "dp"), None), P("dp"))
    return jax.shard_map(local, mesh=mesh, in_specs=in_specs, out_specs=out_specs, check_vma=False)
```
